32 devices in a mesh: groups: 2 (over x), pool: 8 (over z, y), head: 2 (over core).
Axes of the slice: x: 2, y: 2, z: 4, core: 2. Of those that a mesh axis runs over, the one named last changes fastest.
Arguments:
- tokens: bfloat16 [128, 7168], P(('groups', 'pool')), parts along dimension 0, may hold values from -6 to 6
- queries: bfloat16 [128, 64, 576], P(('groups', 'pool'), 'head'), parts along dimension 0, may hold values from -60 to 60
- cache_latent: bfloat16 [128, 512, 576], P(('groups', 'pool')), parts along dimension 0, may hold values from -6 to 6
- page_lists: int32 [128, 4], P(('groups', 'pool')), parts along dimension 0, may hold values from 0 to 7, as said below
- cache_lengths: int32 [128], P(('groups', 'pool')), parts along dimension 0, may hold values from 256 to 512, as said below
- value_up: bfloat16 [2, 32, 512, 128], P('head', 'pool'), may hold values from -0.25 to 0.25
- out_proj: bfloat16 [2, 32, 128, 7168], P('head', 'pool'), may hold values from -0.25 to 0.25
- norm_gain: float32 [7168], replicated, may hold values from 0.1 to 1.9
- expert_ids: int32 [128, 2], P(('groups', 'pool')), parts along dimension 0, may hold values from 0 to 3, all different within a row; in each aligned block of 8 rows (0 to 7, 8 to 15, ...) at most 8 rows name the same one
- route_weights: float32 [128, 2], P(('groups', 'pool')), parts along dimension 0, may hold values from 0.2 to 2
- gate_proj: bfloat16 [8, 7168, 1024], P('pool', None, 'head'), may hold values from -0.0625 to 0.0625
- up_proj: bfloat16 [8, 7168, 1024], P('pool', None, 'head'), may hold values from -0.0625 to 0.0625
- down_proj: bfloat16 [8, 1024, 7168], P('pool', 'head'), may hold values from -0.125 to 0.125
Outputs:
- mixed: bfloat16 [128, 7168], P(('groups', 'pool')), parts along dimension 0
The draws below stay inside these ranges and needn't reach their ends.
There are 2 independent parts, one for each index of `groups`. The reference program is written for one: setup_inputs(seed, part) draws one part's arguments, and reference() takes and returns one part's arrays. A program takes and returns all parts, laid end to end along the dimension named above; an argument that names none is the same for every part. Nothing has to cross between parts.
Inputs may be any that keep to these rules, and one draw needn't show every extreme that they name: `page_lists`: each row names 4 different pages of its stream, page 0 and the page that holds the stream's last cached position among them, and only pages that begin below the stream's cache length. `cache_lengths`: some stream of every part has all 512 positions cached. `expert_ids`: each row names 2 different experts.
All inputs are finite; a program needn't handle non-finite values.
Results may differ from the reference program's by a relative error of at most 0.018.
Values may be sent and summed in bfloat16 or wider, within the bound.
A program may use at most 128 MiB of HBM per device.

```python
import math
import jax
import jax.numpy as jnp
import numpy as np
from jax import lax

D = 7168
FF = 2048
HEADS = 64
LATENT = 512
VDIM = 128
EXPERTS = 4
TOP = 2
STR_DEV = 8
CTX = 512
PAGE = 64
SEL = 4
KDIM = 576
NPAGE = 8
KEYS = 256
SPAN = 2
STREAMS = 64
N_HEAD = 2


def base_cache(key):
    drawn = jax.random.normal(jax.random.fold_in(key, 11), (STREAMS, CTX, KDIM), jnp.float32)
    return jnp.clip(drawn, -6.0, 6.0)


def stream_lengths(key):
    key = jax.random.fold_in(key, 21)
    shorter = jax.random.randint(key, (STREAMS,), 0, CTX // 2 + 1)
    longest = jax.random.randint(jax.random.fold_in(key, 1), (), 0, STREAMS)
    return jnp.where(jnp.arange(STREAMS) == longest, CTX, CTX - shorter).astype(jnp.int32)


def draw_cache_latent(key, part):
    cache = base_cache(key)
    return cache.astype(jnp.bfloat16)


def draw_queries(key, part):
    key = jax.random.fold_in(key, 5)
    query = jnp.clip(jax.random.normal(key, (STREAMS, HEADS, KDIM), jnp.float32), -6.0, 6.0)
    return jnp.clip(query, -60.0, 60.0).astype(jnp.bfloat16)


def draw_cache_lengths(key, part):
    lengths = stream_lengths(key)
    return lengths


def draw_page_lists(key, part):
    lengths = stream_lengths(key)
    key = jax.random.fold_in(key, 9)
    last_page = (lengths - 1) // PAGE
    pages = jnp.arange(NPAGE, dtype=jnp.int32)[None, :]
    ranks = jax.random.randint(key, (STREAMS, NPAGE), 0, 4096) * NPAGE + pages
    ranks = ranks + jnp.where((pages == 0) | (pages == last_page[:, None]), 1 << 24, 0)
    ranks = ranks - jnp.where(pages > last_page[:, None], 1 << 23, 0)
    picked_ranks, chosen = lax.top_k(ranks, SEL)
    return chosen.astype(jnp.int32)


def shard_levels(key, dims, split, low, top_value):
    loudness, own = 1.0, jax.random.fold_in(key, 6)
    for position, shards_of in split:
        steps = jnp.exp(jax.random.uniform(jax.random.fold_in(own, position), (shards_of,), jnp.float32, low / len(split), top_value / len(split)))
        loudness = loudness * jnp.repeat(steps, dims[position] // shards_of).reshape([-1 if axis == position else 1 for axis in range(len(dims))])
    return loudness


def assign_block(key, own, number, rows, number_of, top, most, skew):
    order = jax.random.permutation(key, number_of)
    heavy_load, usual = portions_of(number_of, rows * top, most, skew, True), portions_of(number_of, rows * top, most, skew, False)
    places = jnp.arange(number_of)

    def named(sizes, rotation):
        used = int((sizes > 0).sum())
        fixed = max(1, used // 4)
        shifted = fixed + (places - fixed + rotation * (used - fixed)) % max(1, number_of - fixed)
        return jnp.zeros((number_of,), jnp.int32).at[order[jnp.where(places < fixed, places, shifted)]].set(jnp.asarray(sizes, jnp.int32))

    sizes = jnp.where(number % 4 == 0, named(heavy_load, number // 4), named(usual, number - number // 4 - 1))
    mixed = jax.random.permutation(jax.random.fold_in(own, 3), number_of)
    donor, taker = mixed[0:number_of // 2 * 2:2], mixed[1:number_of // 2 * 2:2]
    slack = jnp.minimum(sizes[donor] - 1, most - sizes[taker]) // 2
    slack = jnp.where((donor == order[0]) | (taker == order[0]) | (sizes[taker] == 0), 0, jnp.maximum(slack, 0))
    shifted = jax.random.randint(jax.random.fold_in(own, 4), (number_of // 2,), 0, 1 << 20) % (slack + 1)
    sizes = sizes.at[donor].add(-shifted).at[taker].add(shifted)
    members = jnp.searchsorted(jnp.cumsum(sizes), jnp.arange(rows * top), side="right").astype(jnp.int32)
    listing = members.reshape(top, rows).T
    listing = listing[jax.random.permutation(jax.random.fold_in(own, 1), rows)]
    rotation = jax.random.randint(jax.random.fold_in(own, 2), (rows, 1), 0, top)
    return jnp.take_along_axis(listing, (jnp.arange(top)[None, :] + rotation) % top, axis=1)


def portions_of(number_of, total, bound, lean, full):
    portions = [(1 << 20) // math.isqrt(standing ** lean) + 1 for standing in range(1, number_of + 1)]
    largest = bound if full else min(bound, max(-(-total // number_of), total * portions[0] // sum(portions)))
    least = 1 if total - largest >= number_of - 1 else 0
    counts, rest = [largest] + [least] * (number_of - 1), total - largest - least * (number_of - 1)
    while rest > 0:
        movable = [i for i in range(1, number_of) if counts[i] < largest] or [i for i in range(1, number_of) if counts[i] < bound]
        whole, remaining = sum([portions[i] for i in movable]), rest
        for i in movable:
            extra = min(bound - counts[i], max(1, remaining * portions[i] // whole), rest)
            counts[i] = counts[i] + extra
            rest = rest - extra
    return np.array(counts)


def gaussian(stream_key, dims, scale, limit, cuts=(), kind=jnp.bfloat16):
    result = scale * jax.random.normal(stream_key, dims, jnp.float32)
    if cuts:
        result = result * shard_levels(stream_key, dims, cuts, -0.22, 0.18)
    return jnp.clip(result, -limit, limit).astype(kind)


def setup_inputs(seed: int = 0, part: int = 0) -> dict:
    seeds = jax.random.split(jax.random.key(seed), 14)
    part_keys = jax.random.split(jax.random.fold_in(seeds[13], part), 14)
    tokens = gaussian(part_keys[0], (STREAMS, D), 1.0, 6.0, ((0, 8),))
    queries = draw_queries(jax.random.fold_in(jax.random.fold_in(seeds[13], part), 71), part)
    cache_latent = draw_cache_latent(jax.random.fold_in(jax.random.fold_in(seeds[13], part), 71), part)
    page_lists = draw_page_lists(jax.random.fold_in(jax.random.fold_in(seeds[13], part), 71), part)
    cache_lengths = draw_cache_lengths(jax.random.fold_in(jax.random.fold_in(seeds[13], part), 71), part)
    value_up = gaussian(seeds[5], (N_HEAD, HEADS // N_HEAD, LATENT, VDIM), LATENT ** -0.5, 0.25, ((0, 2), (1, 8)))
    out_proj = gaussian(seeds[6], (N_HEAD, HEADS // N_HEAD, VDIM, D), (HEADS * VDIM // 16) ** -0.5, 0.25, ((0, 2), (1, 8)))
    norm_gain = jnp.clip(1.0 + 0.18 * jax.random.normal(seeds[7], (D,), jnp.float32), 0.1, 1.9)
    expert_ids_keys = jax.random.split(jax.random.fold_in(part_keys[8], 1), STREAMS // STR_DEV)
    expert_ids_turns = jax.random.permutation(jax.random.fold_in(part_keys[8], 3), STREAMS // STR_DEV)
    expert_ids = jax.vmap(lambda own, number: assign_block(jax.random.fold_in(part_keys[8], 2), own, number, STR_DEV, EXPERTS, TOP, STR_DEV, 2))(expert_ids_keys, expert_ids_turns).reshape((STREAMS, TOP))
    route_weights = jnp.clip(jnp.exp(math.log(2.0) - 2.3025851 * jax.random.uniform(part_keys[9], (STREAMS, TOP), jnp.float32) ** shard_levels(part_keys[9], (STREAMS, TOP), ((0, 8),), -0.2, 0.2)), 0.2, 2.0)
    gate_proj = gaussian(seeds[10], (EXPERTS * SPAN, D, FF // SPAN), D ** -0.5, 0.0625, ((0, 8), (2, 2)))
    up_proj = gaussian(seeds[11], (EXPERTS * SPAN, D, FF // SPAN), D ** -0.5, 0.0625, ((0, 8), (2, 2)))
    down_proj = gaussian(seeds[12], (EXPERTS * SPAN, FF // SPAN, D), FF ** -0.5, 0.125, ((0, 8), (1, 2)))
    return {"tokens": tokens, "queries": queries, "cache_latent": cache_latent, "page_lists": page_lists, "cache_lengths": cache_lengths, "value_up": value_up, "out_proj": out_proj, "norm_gain": norm_gain, "expert_ids": expert_ids, "route_weights": route_weights, "gate_proj": gate_proj, "up_proj": up_proj, "down_proj": down_proj}


softmax_scale = 192 ** (-0.5)

def attend(queries, cache_latent, page_lists, cache_lengths):
    streams = queries.shape[0]
    pages = cache_latent.reshape(streams, NPAGE, PAGE, KDIM)
    picked = jnp.take_along_axis(pages, page_lists[:, :, None, None].astype(jnp.int32), axis=1).reshape(streams, KEYS, KDIM)
    offsets = (page_lists[:, :, None] * PAGE + jnp.arange(PAGE, dtype=jnp.int32)[None, None, :]).reshape(streams, KEYS)
    usable = offsets < cache_lengths[:, None]
    scores = jnp.einsum('shc,skc->shk', queries.astype(jnp.float32), picked.astype(jnp.float32)) * softmax_scale
    scores = jnp.where(usable[:, None, :], scores, -1e+30)
    top = lax.optimization_barrier(jnp.max(scores, axis=-1, keepdims=True))
    weighed = jnp.exp(scores - top) * usable[:, None, :].astype(jnp.float32)
    probs = (weighed / lax.optimization_barrier(jnp.sum(weighed, axis=-1, keepdims=True))).astype(jnp.bfloat16)
    return jnp.einsum('shk,skc->shc', probs.astype(jnp.float32), picked[:, :, :LATENT].astype(jnp.float32)).astype(jnp.bfloat16)

def reference(tokens, queries, cache_latent, page_lists, cache_lengths, value_up, out_proj, norm_gain, expert_ids, route_weights, gate_proj, up_proj, down_proj):
    latent_out = attend(queries, cache_latent, page_lists, cache_lengths)
    head_values = jnp.einsum('shc,hcv->shv', latent_out.astype(jnp.float32), value_up.reshape(HEADS, LATENT, VDIM).astype(jnp.float32)).astype(jnp.bfloat16)
    attn_out = jnp.einsum('shv,hvd->sd', head_values.astype(jnp.float32), out_proj.reshape(HEADS, VDIM, D).astype(jnp.float32))
    residual = tokens.astype(jnp.float32) + attn_out
    scale_back = lax.rsqrt(lax.optimization_barrier(jnp.mean(residual * residual, axis=-1, keepdims=True)) + 1e-06)
    normed = (residual * scale_back * norm_gain[None, :]).astype(jnp.bfloat16)
    groups = SPAN * N_HEAD
    width = FF // groups
    moe_out = jnp.zeros((STREAMS, D), jnp.float32)
    for expert in range(EXPERTS):
        gate_e = gate_proj.reshape(EXPERTS, SPAN, D, FF // SPAN)[expert].transpose(1, 0, 2).reshape(D, FF)
        up_e = up_proj.reshape(EXPERTS, SPAN, D, FF // SPAN)[expert].transpose(1, 0, 2).reshape(D, FF)
        down_e = down_proj.reshape(EXPERTS, SPAN, FF // SPAN, D)[expert].reshape(groups, width, D)
        gate_val = jnp.dot(normed, gate_e, preferred_element_type=jnp.float32)
        up_val = jnp.dot(normed, up_e, preferred_element_type=jnp.float32)
        act = (jax.nn.silu(gate_val) * up_val).astype(jnp.bfloat16)
        partial_out = jnp.einsum('sgf,gfd->sgd', act.reshape(STREAMS, groups, width).astype(jnp.float32), down_e.astype(jnp.float32)).astype(jnp.bfloat16)
        expert_out = lax.optimization_barrier(jnp.sum(partial_out.astype(jnp.float32), axis=1))
        share = lax.optimization_barrier(jnp.sum(jnp.where(expert_ids == expert, route_weights, 0.0), axis=1))
        moe_out = moe_out + share[:, None] * expert_out
    return (residual + moe_out).astype(jnp.bfloat16)
```

```python
import functools

import jax
import jax.numpy as jnp
from jax import lax
from jax.experimental import pallas as pl
from jax.experimental.pallas import tpu as pltpu
from jax.sharding import PartitionSpec as P

LATENT = 512
EXPERTS = 4
PAGE = 64
CHUNKS = 2
SCALE = 192 ** (-0.5)
MESH = pl.DeviceIdType.MESH
BF16 = jnp.bfloat16
F32 = jnp.float32


def log2(n):
    assert n & (n - 1) == 0
    return n.bit_length() - 1


def dot(a, b):
    return jnp.dot(a, b, preferred_element_type=F32)


def kernel(
    pool,
    tok_hbm, q_hbm, cache_hbm, pages_ref, lens_ref, vu_hbm, op_hbm, gain_ref, ids_ref, rw_ref,
    g_hbm, u_hbm, d_hbm,
    out_ref,
    tok, q, cache, vu, op, gw, uw, dw,
    scores, lat, a_buf, a_recv, x_buf, x_recv, r_buf, r_recv, c_recv, resid, o_buf,
    k_sem, w_sem, a_s, a_r, x_s, x_r, r_s, r_r, c_s, c_r, f_s, f_r, o_s, o_r,
):
    p = lax.axis_index("pool")
    h = lax.axis_index("head")
    oh = 1 - h
    ns, nh, _ = q.shape
    ctx = cache.shape[1]
    hh_n = vu.shape[0]
    width = tok.shape[1]
    half = width // 2
    ck = half // CHUNKS
    cq = ck // 2
    rows = ns * nh
    toks = pool * ns
    block_w = CHUNKS * cq

    load_q = pltpu.make_async_copy(q_hbm, q, w_sem.at[0])
    load_q.start()
    load_k = [pltpu.make_async_copy(cache_hbm.at[s], cache.at[s], k_sem.at[s]) for s in range(ns)]
    for copy in load_k:
        copy.start()
    load_vu = pltpu.make_async_copy(vu_hbm, vu, w_sem.at[1])
    load_op = pltpu.make_async_copy(op_hbm, op, w_sem.at[2])
    load_tok = pltpu.make_async_copy(tok_hbm, tok, w_sem.at[3])
    load_g = pltpu.make_async_copy(g_hbm, gw, w_sem.at[4])
    load_u = pltpu.make_async_copy(u_hbm, uw, w_sem.at[5])
    load_d = pltpu.make_async_copy(d_hbm, dw, w_sem.at[6])
    for copy in (load_vu, load_op, load_tok, load_g, load_u, load_d):
        copy.start()

    def peer(d):
        return lax.rem(p + d, pool)

    def source(d):
        return lax.rem(p + pool - d, pool)

    barrier = pltpu.get_barrier_semaphore()

    def greet(d, carry):
        pl.semaphore_signal(barrier, inc=1, device_id={"pool": peer(d)}, device_id_type=MESH)
        return carry

    lax.fori_loop(1, pool, greet, 0)
    pl.semaphore_signal(barrier, inc=1, device_id={"head": oh}, device_id_type=MESH)

    def to_pool(src, dst, send, recv, to):
        return pltpu.make_async_remote_copy(
            src_ref=src, dst_ref=dst, send_sem=send, recv_sem=recv,
            device_id={"pool": to}, device_id_type=MESH,
        )

    def to_core(src, dst, send, recv):
        return pltpu.make_async_remote_copy(
            src_ref=src, dst_ref=dst, send_sem=send, recv_sem=recv,
            device_id={"head": oh}, device_id_type=MESH,
        )

    def each(body):
        def step(d, carry):
            body(d)
            return carry

        lax.fori_loop(1, pool, step, 0)

    pos = lax.broadcasted_iota(jnp.int32, (ns, ctx), 1)
    page = pos >> log2(PAGE)
    listed = pages_ref[:, 0:1] == page
    for j in range(1, pages_ref.shape[1]):
        listed = listed | (pages_ref[:, j : j + 1] == page)
    usable = jnp.where(listed & (pos < lens_ref[:, 0:1]), 1.0, 0.0)
    load_q.wait()
    for s in range(ns):
        load_k[s].wait()
        scores[s] = lax.dot_general(
            q[s], cache[s], (((1,), (1,)), ((), ())), preferred_element_type=F32
        )
    for s in range(ns):
        keep = usable[s : s + 1, :] > 0.5
        sc = jnp.where(keep, scores[s] * SCALE, -1e30)
        top = jnp.max(sc, axis=-1, keepdims=True)
        weighed = jnp.where(keep, jnp.exp(sc - top), 0.0)
        probs = (weighed / jnp.sum(weighed, axis=-1, keepdims=True)).astype(BF16)
        lat[s * nh : (s + 1) * nh, :] = dot(probs, cache[s, :, :LATENT]).astype(BF16)

    per = ns * hh_n
    ri = lax.broadcasted_iota(jnp.int32, (rows, 1), 0)
    rest = ri & (per - 1)
    origin = (rest >> log2(hh_n)) * nh + (ri >> log2(per)) * hh_n + (rest & (hh_n - 1))
    ci = lax.broadcasted_iota(jnp.int32, (rows, rows), 1)
    perm = jnp.where(ci == origin, 1.0, 0.0).astype(BF16)
    a_buf[...] = dot(perm, lat[...]).reshape(pool, per, LATENT).astype(BF16)
    pl.semaphore_wait(barrier, pool)

    def a_copy(d, slot):
        return to_pool(a_buf.at[peer(d)], a_recv.at[slot], a_s.at[d], a_r.at[d], peer(d))

    each(lambda d: a_copy(d, p).start())
    a_recv[p] = a_buf[p]
    load_vu.wait()
    each(lambda d: a_copy(d, source(d)).wait_recv())
    got = a_recv[...].astype(F32).reshape(rows, LATENT).astype(BF16)
    values = []
    ti = lax.broadcasted_iota(jnp.int32, (toks, rows), 0)
    tj = lax.broadcasted_iota(jnp.int32, (toks, rows), 1)
    for hh in range(hh_n):
        if hh_n > 1:
            pick = jnp.where(tj == ti * hh_n + hh, 1.0, 0.0).astype(BF16)
            mine = dot(pick, got).astype(BF16)
        else:
            mine = got
        values.append(dot(mine, vu[hh]).astype(BF16))
    head_values = jnp.concatenate(values, axis=1) if hh_n > 1 else values[0]

    def x_copy(i, c):
        return to_core(x_buf.at[i, c], x_recv.at[i, c], x_s.at[i, c], x_r.at[i, c])

    def r_copy(i, c, d, slot):
        return to_pool(
            r_buf.at[i, c, peer(d)], r_recv.at[i, c, slot], r_s.at[i, c, d], r_r.at[i, c, d], peer(d)
        )

    def columns(side, c, j=0, size=ck):
        return pl.ds(pl.multiple_of(side * half + (c * ck + j * cq), 128), size)

    def reduce_send(i, lhs, weights, by):
        for c in range(CHUNKS):
            v = dot(lhs, weights[:, columns(oh, c)])
            if by is not None:
                v = v * by
            x_buf[i, c] = v.astype(BF16)
            x_copy(i, c).start()
        for c in range(CHUNKS):
            v = dot(lhs, weights[:, columns(h, c)])
            if by is not None:
                v = v * by
            x_copy(i, c).wait_recv()
            v = v + x_recv[i, c].astype(F32)
            low = v[:, :cq].reshape(pool, ns, cq)
            high = v[:, cq:].reshape(pool, ns, cq)
            r_buf[i, c] = jnp.concatenate([low, high], axis=1).astype(BF16)
            each(lambda d: r_copy(i, c, d, p).start())
            r_recv[i, c, p] = r_buf[i, c, p]

    def reduced(i, c):
        each(lambda d: r_copy(i, c, d, source(d)).wait_recv())
        return jnp.sum(r_recv[i, c].astype(F32), axis=0)

    load_op.wait()
    reduce_send(0, head_values, op, None)

    load_tok.wait()
    squares = jnp.zeros((ns, 1), F32)
    for c in range(CHUNKS):
        total = reduced(0, c)
        tokens = jnp.concatenate(
            [tok[:, columns(h, c, j, cq)].astype(F32) for j in range(2)], axis=0
        )
        gain = jnp.concatenate(
            [jnp.broadcast_to(gain_ref[0:1, columns(h, c, j, cq)], (ns, cq)) for j in range(2)], axis=0
        )
        res = tokens + total
        resid[c] = res
        both = jnp.sum(res * res, axis=-1, keepdims=True)
        squares = squares + both[:ns] + both[ns:]
        c_recv[h, p, :, c * cq : (c + 1) * cq] = (res * gain).astype(BF16)
    lane = lax.broadcasted_iota(jnp.int32, (ns, 128), 1)
    extra = jnp.broadcast_to(squares, (ns, 128))
    extra = jnp.where(lane < EXPERTS, 0.0, extra)
    for k in range(ids_ref.shape[1]):
        extra = extra + jnp.where(lane == ids_ref[:, k : k + 1], rw_ref[:, k : k + 1], 0.0)
    upper = extra.astype(BF16).astype(F32)
    c_recv[h, p, :, block_w:] = jnp.concatenate([upper, extra - upper], axis=0).astype(BF16)

    def c_copy(d, slot):
        return to_pool(c_recv.at[h, slot], c_recv.at[h, slot], c_s.at[d], c_r.at[d], peer(d))

    def f_copy(d, side, slot):
        return to_core(c_recv.at[side, slot], c_recv.at[side, slot], f_s.at[d], f_r.at[d])

    each(lambda d: c_copy(d, p).start())
    f_copy(0, h, p).start()
    load_g.wait()
    load_u.wait()

    def pass_on(d):
        c_copy(d, source(d)).wait_recv()
        f_copy(d, h, source(d)).start()

    each(pass_on)

    def project(side):
        gate = up = None
        for c in range(CHUNKS):
            part = c_recv[side, :, :, c * cq : (c + 1) * cq].astype(F32)
            x = jnp.concatenate(
                [part[:, j * ns : (j + 1) * ns].reshape(toks, cq) for j in range(2)], axis=1
            ).astype(BF16)
            g = dot(x, gw[columns(side, c), :])
            u = dot(x, uw[columns(side, c), :])
            gate = g if gate is None else gate + g
            up = u if up is None else up + u
        part = c_recv[side, :, :, block_w:].astype(F32)
        return gate, up, (part[:, :ns] + part[:, ns:]).reshape(toks, 128)

    gate0, up0, extra0 = project(h)
    f_copy(0, oh, p).wait_recv()
    each(lambda d: f_copy(d, oh, source(d)).wait_recv())
    gate1, up1, extra1 = project(oh)
    lane = lax.broadcasted_iota(jnp.int32, (toks, 128), 1)
    expert = p // (pool // EXPERTS)
    share = jnp.sum(jnp.where(lane == expert, extra0, 0.0), axis=-1, keepdims=True)
    squares = jnp.sum(jnp.where(lane == EXPERTS, extra0 + extra1, 0.0), axis=-1, keepdims=True)
    back = lax.rsqrt(squares / width + 1e-06)
    gate = (gate0 + gate1) * back
    up = (up0 + up1) * back
    act = (gate / (1.0 + jnp.exp(-gate)) * up).astype(BF16)

    load_d.wait()
    reduce_send(1, act, dw, share)
    for c in range(CHUNKS):
        o_buf[h, c] = (resid[c] + reduced(1, c)).astype(BF16)

    def o_copy(side):
        return to_core(o_buf.at[side], o_buf.at[side], o_s.at[0], o_r.at[0])

    o_copy(h).start()

    def sent(d):
        a_copy(d, p).wait_send()
        c_copy(d, p).wait_send()
        f_copy(d, h, source(d)).wait_send()
        for i in range(2):
            for c in range(CHUNKS):
                r_copy(i, c, d, p).wait_send()

    each(sent)
    f_copy(0, h, p).wait_send()
    for i in range(2):
        for c in range(CHUNKS):
            x_copy(i, c).wait_send()
    o_copy(oh).wait_recv()
    for side in range(2):
        for c in range(CHUNKS):
            part = o_buf[side, c].astype(F32)
            for j in range(2):
                at = side * half + c * ck + j * cq
                out_ref[:, at : at + cq] = part[j * ns : (j + 1) * ns].astype(BF16)
    o_copy(h).wait_send()


def per_device(
    pool,
    tokens, queries, cache_latent, page_lists, cache_lengths, value_up, out_proj, norm_gain,
    expert_ids, route_weights, gate_proj, up_proj, down_proj,
):
    ns, width = tokens.shape
    _, nh, kdim = queries.shape
    ctx = cache_latent.shape[1]
    _, hh_n, latent, vdim = value_up.shape
    hidden = gate_proj.shape[2]
    half = width // 2
    ck = half // CHUNKS
    cq = ck // 2
    toks = pool * ns
    dma = pltpu.SemaphoreType.DMA
    anywhere = pl.BlockSpec(memory_space=pl.ANY)
    vmem = pl.BlockSpec(memory_space=pltpu.VMEM)
    return pl.pallas_call(
        functools.partial(kernel, pool),
        out_shape=jax.ShapeDtypeStruct((ns, width), BF16),
        in_specs=[
            anywhere, anywhere, anywhere, vmem, vmem, anywhere, anywhere, vmem, vmem, vmem,
            anywhere, anywhere, anywhere,
        ],
        out_specs=vmem,
        scratch_shapes=[
            pltpu.VMEM((ns, width), BF16),
            pltpu.VMEM((ns, nh, kdim), BF16),
            pltpu.VMEM((ns, ctx, kdim), BF16),
            pltpu.VMEM((hh_n, latent, vdim), BF16),
            pltpu.VMEM((hh_n * vdim, width), BF16),
            pltpu.VMEM((width, hidden), BF16),
            pltpu.VMEM((width, hidden), BF16),
            pltpu.VMEM((hidden, width), BF16),
            pltpu.VMEM((ns, nh, ctx), F32),
            pltpu.VMEM((ns * nh, latent), BF16),
            pltpu.VMEM((pool, ns * hh_n, latent), BF16),
            pltpu.VMEM((pool, ns * hh_n, latent), BF16),
            pltpu.VMEM((2, CHUNKS, toks, ck), BF16),
            pltpu.VMEM((2, CHUNKS, toks, ck), BF16),
            pltpu.VMEM((2, CHUNKS, pool, 2 * ns, cq), BF16),
            pltpu.VMEM((2, CHUNKS, pool, 2 * ns, cq), BF16),
            pltpu.VMEM((2, pool, 2 * ns, CHUNKS * cq + 128), BF16),
            pltpu.VMEM((CHUNKS, 2 * ns, cq), F32),
            pltpu.VMEM((2, CHUNKS, 2 * ns, cq), BF16),
            dma((ns,)), dma((7,)),
            dma((pool,)), dma((pool,)),
            dma((2, CHUNKS)), dma((2, CHUNKS)),
            dma((2, CHUNKS, pool)), dma((2, CHUNKS, pool)),
            dma((pool,)), dma((pool,)),
            dma((pool,)), dma((pool,)),
            dma((1,)), dma((1,)),
        ],
        compiler_params=pltpu.CompilerParams(
            collective_id=0, has_side_effects=True, vmem_limit_bytes=60 * 1024 * 1024
        ),
        name="decode_layer",
    )(
        tokens, queries, cache_latent, page_lists, cache_lengths.reshape(ns, 1),
        value_up.reshape(hh_n, latent, vdim), out_proj.reshape(hh_n * vdim, width),
        norm_gain.reshape(1, width), expert_ids, route_weights,
        gate_proj.reshape(width, hidden), up_proj.reshape(width, hidden),
        down_proj.reshape(hidden, width),
    )


def solution(mesh):
    return jax.shard_map(
        functools.partial(per_device, mesh.shape["pool"]),
        mesh=mesh,
        in_specs=(
            P(("groups", "pool"), None),
            P(("groups", "pool"), "head", None),
            P(("groups", "pool"), None, None),
            P(("groups", "pool"), None),
            P(("groups", "pool")),
            P("head", "pool", None, None),
            P("head", "pool", None, None),
            P(),
            P(("groups", "pool"), None),
            P(("groups", "pool"), None),
            P("pool", None, "head"),
            P("pool", None, "head"),
            P("pool", "head", None),
        ),
        out_specs=P(("groups", "pool"), None),
        check_vma=False,
    )
```

```python
import functools

import jax
import jax.numpy as jnp
from jax import lax
from jax.experimental import pallas as pl
from jax.experimental.pallas import tpu as pltpu
from jax.sharding import PartitionSpec as P

LATENT = 512
EXPERTS = 4
PAGE = 64
CHUNKS = 2
SCALE = 192 ** (-0.5)
MESH = pl.DeviceIdType.MESH
BF16 = jnp.bfloat16
F32 = jnp.float32


def log2(n):
    assert n & (n - 1) == 0
    return n.bit_length() - 1


def dot(a, b):
    return jnp.dot(a, b, preferred_element_type=F32)


def kernel(
    pool,
    tok_hbm, q_hbm, cache_hbm, pages_ref, lens_ref, vu_hbm, op_hbm, gain_ref, ids_ref, rw_ref,
    g_hbm, u_hbm, d_hbm,
    out_ref,
    tok, q, cache, vu, op, gw, uw, dw,
    scores, lat, a_buf, a_recv, x_buf, x_recv, r_buf, r_recv, c_recv, resid, o_buf,
    k_sem, w_sem, a_s, a_r, x_s, x_r, r_s, r_r, c_s, c_r, f_s, f_r, o_s, o_r,
):
    p = lax.axis_index("pool")
    h = lax.axis_index("head")
    oh = 1 - h
    ns, nh, _ = q.shape
    ctx = cache.shape[2]
    hh_n = vu.shape[0]
    width = tok.shape[1]
    half = width // 2
    ck = half // CHUNKS
    cq = ck // 2
    rows = ns * nh
    toks = pool * ns
    block_w = CHUNKS * cq

    load_q = pltpu.make_async_copy(q_hbm, q, w_sem.at[0])
    load_q.start()
    load_k = [pltpu.make_async_copy(cache_hbm.at[s], cache.at[s], k_sem.at[s]) for s in range(ns)]
    for copy in load_k:
        copy.start()
    load_vu = pltpu.make_async_copy(vu_hbm, vu, w_sem.at[1])
    load_op = pltpu.make_async_copy(op_hbm, op, w_sem.at[2])
    load_tok = pltpu.make_async_copy(tok_hbm, tok, w_sem.at[3])
    load_g = pltpu.make_async_copy(g_hbm, gw, w_sem.at[4])
    load_u = pltpu.make_async_copy(u_hbm, uw, w_sem.at[5])
    load_d = pltpu.make_async_copy(d_hbm, dw, w_sem.at[6])
    for copy in (load_vu, load_op, load_tok, load_g, load_u, load_d):
        copy.start()

    def peer(d):
        return lax.rem(p + d, pool)

    def source(d):
        return lax.rem(p + pool - d, pool)

    barrier = pltpu.get_barrier_semaphore()

    def greet(d, carry):
        pl.semaphore_signal(barrier, inc=1, device_id={"pool": peer(d)}, device_id_type=MESH)
        return carry

    lax.fori_loop(1, pool, greet, 0)
    pl.semaphore_signal(barrier, inc=1, device_id={"head": oh}, device_id_type=MESH)

    def to_pool(src, dst, send, recv, to):
        return pltpu.make_async_remote_copy(
            src_ref=src, dst_ref=dst, send_sem=send, recv_sem=recv,
            device_id={"pool": to}, device_id_type=MESH,
        )

    def to_core(src, dst, send, recv):
        return pltpu.make_async_remote_copy(
            src_ref=src, dst_ref=dst, send_sem=send, recv_sem=recv,
            device_id={"head": oh}, device_id_type=MESH,
        )

    def each(body):
        def step(d, carry):
            body(d)
            return carry

        lax.fori_loop(1, pool, step, 0)

    pos = lax.broadcasted_iota(jnp.int32, (ns, ctx), 1)
    page = pos >> log2(PAGE)
    eye = lax.broadcasted_iota(jnp.int32, (ns, ns), 0) == lax.broadcasted_iota(jnp.int32, (ns, ns), 1)

    def column(row):
        return jnp.sum(jnp.where(eye, row, 0.0), axis=-1, keepdims=True)

    def whole(row):
        return column(row.astype(F32)).astype(jnp.int32)

    listed = whole(pages_ref[0:1, :]) == page
    for j in range(1, pages_ref.shape[0]):
        listed = listed | (whole(pages_ref[j : j + 1, :]) == page)
    usable = jnp.where(listed & (pos < whole(lens_ref[0:1, :])), 1.0, 0.0)
    load_q.wait()
    for s in range(ns):
        load_k[s].wait()
        scores[s] = dot(q[s], cache[s])
    for s in range(ns):
        keep = usable[s : s + 1, :] > 0.5
        sc = jnp.where(keep, scores[s] * SCALE, -1e30)
        top = jnp.max(sc, axis=-1, keepdims=True)
        weighed = jnp.where(keep, jnp.exp(sc - top), 0.0)
        probs = (weighed / jnp.sum(weighed, axis=-1, keepdims=True)).astype(BF16)
        lat[s * nh : (s + 1) * nh, :] = lax.dot_general(
            probs, cache[s, :LATENT, :], (((1,), (1,)), ((), ())), preferred_element_type=F32
        ).astype(BF16)

    per = ns * hh_n
    ri = lax.broadcasted_iota(jnp.int32, (rows, 1), 0)
    rest = ri & (per - 1)
    origin = (rest >> log2(hh_n)) * nh + (ri >> log2(per)) * hh_n + (rest & (hh_n - 1))
    ci = lax.broadcasted_iota(jnp.int32, (rows, rows), 1)
    perm = jnp.where(ci == origin, 1.0, 0.0).astype(BF16)
    a_buf[...] = dot(perm, lat[...]).reshape(pool, per, LATENT).astype(BF16)
    pl.semaphore_wait(barrier, pool)

    def a_copy(d, slot):
        return to_pool(a_buf.at[peer(d)], a_recv.at[slot], a_s.at[d], a_r.at[d], peer(d))

    each(lambda d: a_copy(d, p).start())
    a_recv[p] = a_buf[p]
    load_vu.wait()
    each(lambda d: a_copy(d, source(d)).wait_recv())
    got = a_recv[...].astype(F32).reshape(rows, LATENT).astype(BF16)
    values = []
    ti = lax.broadcasted_iota(jnp.int32, (toks, rows), 0)
    tj = lax.broadcasted_iota(jnp.int32, (toks, rows), 1)
    for hh in range(hh_n):
        if hh_n > 1:
            pick = jnp.where(tj == ti * hh_n + hh, 1.0, 0.0).astype(BF16)
            mine = dot(pick, got).astype(BF16)
        else:
            mine = got
        values.append(dot(mine, vu[hh]).astype(BF16))
    head_values = jnp.concatenate(values, axis=1) if hh_n > 1 else values[0]

    def x_copy(i, c):
        return to_core(x_buf.at[i, c], x_recv.at[i, c], x_s.at[i, c], x_r.at[i, c])

    def r_copy(i, c, d, slot):
        return to_pool(
            r_buf.at[i, c, peer(d)], r_recv.at[i, c, slot], r_s.at[i, c, d], r_r.at[i, c, d], peer(d)
        )

    def columns(side, c, j=0, size=ck):
        return pl.ds(pl.multiple_of(side * half + (c * ck + j * cq), 128), size)

    def reduce_send(i, lhs, weights, by):
        for c in range(CHUNKS):
            v = dot(lhs, weights[:, columns(oh, c)])
            if by is not None:
                v = v * by
            x_buf[i, c] = v.astype(BF16)
            x_copy(i, c).start()
        for c in range(CHUNKS):
            v = dot(lhs, weights[:, columns(h, c)])
            if by is not None:
                v = v * by
            x_copy(i, c).wait_recv()
            v = v + x_recv[i, c].astype(F32)
            low = v[:, :cq].reshape(pool, ns, cq)
            high = v[:, cq:].reshape(pool, ns, cq)
            r_buf[i, c] = jnp.concatenate([low, high], axis=1).astype(BF16)
            each(lambda d: r_copy(i, c, d, p).start())
            r_recv[i, c, p] = r_buf[i, c, p]

    def reduced(i, c):
        each(lambda d: r_copy(i, c, d, source(d)).wait_recv())
        return jnp.sum(r_recv[i, c].astype(F32), axis=0)

    load_op.wait()
    reduce_send(0, head_values, op, None)

    load_tok.wait()
    squares = jnp.zeros((ns, 1), F32)
    for c in range(CHUNKS):
        total = reduced(0, c)
        tokens = jnp.concatenate(
            [tok[:, columns(h, c, j, cq)].astype(F32) for j in range(2)], axis=0
        )
        gain = jnp.concatenate(
            [jnp.broadcast_to(gain_ref[0:1, columns(h, c, j, cq)], (ns, cq)) for j in range(2)], axis=0
        )
        res = tokens + total
        resid[c] = res
        both = jnp.sum(res * res, axis=-1, keepdims=True)
        squares = squares + both[:ns] + both[ns:]
        c_recv[h, p, :, c * cq : (c + 1) * cq] = (res * gain).astype(BF16)
    lane = lax.broadcasted_iota(jnp.int32, (ns, 128), 1)
    extra = jnp.broadcast_to(squares, (ns, 128))
    extra = jnp.where(lane < EXPERTS, 0.0, extra)
    for k in range(ids_ref.shape[0]):
        routed = lane == whole(ids_ref[k : k + 1, :])
        extra = extra + jnp.where(routed, column(rw_ref[k : k + 1, :]), 0.0)
    upper = extra.astype(BF16).astype(F32)
    c_recv[h, p, :, block_w:] = jnp.concatenate([upper, extra - upper], axis=0).astype(BF16)

    def c_copy(d, slot):
        return to_pool(c_recv.at[h, slot], c_recv.at[h, slot], c_s.at[d], c_r.at[d], peer(d))

    def f_copy(d, side, slot):
        return to_core(c_recv.at[side, slot], c_recv.at[side, slot], f_s.at[d], f_r.at[d])

    each(lambda d: c_copy(d, p).start())
    f_copy(0, h, p).start()
    load_g.wait()
    load_u.wait()

    def pass_on(d):
        c_copy(d, source(d)).wait_recv()
        f_copy(d, h, source(d)).start()

    each(pass_on)

    def project(side):
        gate = up = None
        for c in range(CHUNKS):
            part = c_recv[side, :, :, c * cq : (c + 1) * cq].astype(F32)
            x = jnp.concatenate(
                [part[:, j * ns : (j + 1) * ns].reshape(toks, cq) for j in range(2)], axis=1
            ).astype(BF16)
            g = dot(x, gw[columns(side, c), :])
            u = dot(x, uw[columns(side, c), :])
            gate = g if gate is None else gate + g
            up = u if up is None else up + u
        part = c_recv[side, :, :, block_w:].astype(F32)
        return gate, up, (part[:, :ns] + part[:, ns:]).reshape(toks, 128)

    gate0, up0, extra0 = project(h)
    f_copy(0, oh, p).wait_recv()
    each(lambda d: f_copy(d, oh, source(d)).wait_recv())
    gate1, up1, extra1 = project(oh)
    lane = lax.broadcasted_iota(jnp.int32, (toks, 128), 1)
    expert = p // (pool // EXPERTS)
    share = jnp.sum(jnp.where(lane == expert, extra0, 0.0), axis=-1, keepdims=True)
    squares = jnp.sum(jnp.where(lane == EXPERTS, extra0 + extra1, 0.0), axis=-1, keepdims=True)
    back = lax.rsqrt(squares / width + 1e-06)
    gate = (gate0 + gate1) * back
    up = (up0 + up1) * back
    act = (gate / (1.0 + jnp.exp(-gate)) * up).astype(BF16)

    load_d.wait()
    reduce_send(1, act, dw, share)
    for c in range(CHUNKS):
        o_buf[h, c] = (resid[c] + reduced(1, c)).astype(BF16)

    def o_copy(side):
        return to_core(o_buf.at[side], o_buf.at[side], o_s.at[0], o_r.at[0])

    o_copy(h).start()

    def sent(d):
        a_copy(d, p).wait_send()
        c_copy(d, p).wait_send()
        f_copy(d, h, source(d)).wait_send()
        for i in range(2):
            for c in range(CHUNKS):
                r_copy(i, c, d, p).wait_send()

    each(sent)
    f_copy(0, h, p).wait_send()
    for i in range(2):
        for c in range(CHUNKS):
            x_copy(i, c).wait_send()
    o_copy(oh).wait_recv()
    for side in range(2):
        for c in range(CHUNKS):
            part = o_buf[side, c].astype(F32)
            for j in range(2):
                at = side * half + c * ck + j * cq
                out_ref[:, at : at + cq] = part[j * ns : (j + 1) * ns].astype(BF16)
    o_copy(h).wait_send()


def per_device(
    pool,
    tokens, queries, cache_latent, page_lists, cache_lengths, value_up, out_proj, norm_gain,
    expert_ids, route_weights, gate_proj, up_proj, down_proj,
):
    ns, width = tokens.shape
    _, nh, kdim = queries.shape
    ctx = cache_latent.shape[1]
    _, hh_n, latent, vdim = value_up.shape
    hidden = gate_proj.shape[2]
    half = width // 2
    ck = half // CHUNKS
    cq = ck // 2
    toks = pool * ns
    dma = pltpu.SemaphoreType.DMA
    anywhere = pl.BlockSpec(memory_space=pl.ANY)
    vmem = pl.BlockSpec(memory_space=pltpu.VMEM)
    return pl.pallas_call(
        functools.partial(kernel, pool),
        out_shape=jax.ShapeDtypeStruct((ns, width), BF16),
        in_specs=[
            anywhere, anywhere, anywhere, vmem, vmem, anywhere, anywhere, vmem, vmem, vmem,
            anywhere, anywhere, anywhere,
        ],
        out_specs=vmem,
        scratch_shapes=[
            pltpu.VMEM((ns, width), BF16),
            pltpu.VMEM((ns, nh, kdim), BF16),
            pltpu.VMEM((ns, kdim, ctx), BF16),
            pltpu.VMEM((hh_n, latent, vdim), BF16),
            pltpu.VMEM((hh_n * vdim, width), BF16),
            pltpu.VMEM((width, hidden), BF16),
            pltpu.VMEM((width, hidden), BF16),
            pltpu.VMEM((hidden, width), BF16),
            pltpu.VMEM((ns, nh, ctx), F32),
            pltpu.VMEM((ns * nh, latent), BF16),
            pltpu.VMEM((pool, ns * hh_n, latent), BF16),
            pltpu.VMEM((pool, ns * hh_n, latent), BF16),
            pltpu.VMEM((2, CHUNKS, toks, ck), BF16),
            pltpu.VMEM((2, CHUNKS, toks, ck), BF16),
            pltpu.VMEM((2, CHUNKS, pool, 2 * ns, cq), BF16),
            pltpu.VMEM((2, CHUNKS, pool, 2 * ns, cq), BF16),
            pltpu.VMEM((2, pool, 2 * ns, CHUNKS * cq + 128), BF16),
            pltpu.VMEM((CHUNKS, 2 * ns, cq), F32),
            pltpu.VMEM((2, CHUNKS, 2 * ns, cq), BF16),
            dma((ns,)), dma((7,)),
            dma((pool,)), dma((pool,)),
            dma((2, CHUNKS)), dma((2, CHUNKS)),
            dma((2, CHUNKS, pool)), dma((2, CHUNKS, pool)),
            dma((pool,)), dma((pool,)),
            dma((pool,)), dma((pool,)),
            dma((1,)), dma((1,)),
        ],
        compiler_params=pltpu.CompilerParams(
            collective_id=0, has_side_effects=True, vmem_limit_bytes=60 * 1024 * 1024
        ),
        name="decode_layer",
    )(
        tokens, queries, jnp.swapaxes(cache_latent, 1, 2), page_lists.T, cache_lengths.reshape(1, ns),
        value_up.reshape(hh_n, latent, vdim), out_proj.reshape(hh_n * vdim, width),
        norm_gain.reshape(1, width), expert_ids.T, route_weights.T,
        gate_proj.reshape(width, hidden), up_proj.reshape(width, hidden),
        down_proj.reshape(hidden, width),
    )


def solution(mesh):
    return jax.shard_map(
        functools.partial(per_device, mesh.shape["pool"]),
        mesh=mesh,
        in_specs=(
            P(("groups", "pool"), None),
            P(("groups", "pool"), "head", None),
            P(("groups", "pool"), None, None),
            P(("groups", "pool"), None),
            P(("groups", "pool")),
            P("head", "pool", None, None),
            P("head", "pool", None, None),
            P(),
            P(("groups", "pool"), None),
            P(("groups", "pool"), None),
            P("pool", None, "head"),
            P("pool", None, "head"),
            P("pool", "head", None),
        ),
        out_specs=P(("groups", "pool"), None),
        check_vma=False,
    )
```

```python
import functools

import jax
import jax.numpy as jnp
from jax import lax
from jax.experimental import pallas as pl
from jax.experimental.pallas import tpu as pltpu
from jax.sharding import PartitionSpec as P

LATENT = 512
EXPERTS = 4
PAGE = 64
CHUNKS = 7
SCALE = 192 ** (-0.5)
MESH = pl.DeviceIdType.MESH
BF16 = jnp.bfloat16
F32 = jnp.float32


def log2(n):
    assert n & (n - 1) == 0
    return n.bit_length() - 1


def dot(a, b):
    return jnp.dot(a, b, preferred_element_type=F32)


def kernel(
    pool,
    tok_hbm, q_hbm, cache_hbm, pages_ref, lens_ref, vu_hbm, op_hbm, gain_ref, ids_ref, rw_ref,
    g_hbm, u_hbm, d_hbm,
    out_ref,
    tok, q, cache, vu, op, gw, uw, dw,
    scores, lat, a_buf, a_recv, x_buf, x_recv, y_buf, y_recv, r_buf, r_recv, c_recv, resid, o_buf,
    k_sem, w_sem, a_s, a_r, x_s, x_r, y_s, y_r, r_s, r_r, c_s, c_r,
    g_s, g_r, f_s, f_r, o_s, o_r,
):
    p = lax.axis_index("pool")
    h = lax.axis_index("head")
    oh = 1 - h
    lines = pool // 2
    z = p // 2
    y = lax.rem(p, 2)
    beside = z * 2 + 1 - y
    ns, nh, _ = q.shape
    ctx = cache.shape[2]
    hh_n = vu.shape[0]
    width = tok.shape[1]
    half = width // 2
    ck = half // CHUNKS
    cq = ck // 2
    rows = ns * nh
    toks = pool * ns
    block_w = CHUNKS * cq

    load_q = pltpu.make_async_copy(q_hbm, q, w_sem.at[0])
    load_q.start()
    load_k = [pltpu.make_async_copy(cache_hbm.at[s], cache.at[s], k_sem.at[s]) for s in range(ns)]
    for copy in load_k:
        copy.start()
    load_vu = pltpu.make_async_copy(vu_hbm, vu, w_sem.at[1])
    load_op = pltpu.make_async_copy(op_hbm, op, w_sem.at[2])
    load_tok = pltpu.make_async_copy(tok_hbm, tok, w_sem.at[3])
    load_g = pltpu.make_async_copy(g_hbm, gw, w_sem.at[4])
    load_u = pltpu.make_async_copy(u_hbm, uw, w_sem.at[5])
    load_d = pltpu.make_async_copy(d_hbm, dw, w_sem.at[6])
    for copy in (load_vu, load_op, load_tok):
        copy.start()

    def peer(d):
        return lax.rem(p + d, pool)

    def source(d):
        return lax.rem(p + pool - d, pool)

    barrier = pltpu.get_barrier_semaphore()

    def greet(d, carry):
        pl.semaphore_signal(barrier, inc=1, device_id={"pool": peer(d)}, device_id_type=MESH)
        return carry

    lax.fori_loop(1, pool, greet, 0)
    pl.semaphore_signal(barrier, inc=1, device_id={"head": oh}, device_id_type=MESH)

    def to_pool(src, dst, send, recv, to):
        return pltpu.make_async_remote_copy(
            src_ref=src, dst_ref=dst, send_sem=send, recv_sem=recv,
            device_id={"pool": to}, device_id_type=MESH,
        )

    def to_core(src, dst, send, recv):
        return pltpu.make_async_remote_copy(
            src_ref=src, dst_ref=dst, send_sem=send, recv_sem=recv,
            device_id={"head": oh}, device_id_type=MESH,
        )

    def each(body, low=1, high=pool):
        def step(d, carry):
            body(d)
            return carry

        lax.fori_loop(low, high, step, 0)

    def ahead(d):
        return lax.rem(z + d, lines)

    def behind(d):
        return lax.rem(z + lines - d, lines)

    pos = lax.broadcasted_iota(jnp.int32, (ns, ctx), 1)
    page = pos >> log2(PAGE)
    eye = lax.broadcasted_iota(jnp.int32, (ns, ns), 0) == lax.broadcasted_iota(jnp.int32, (ns, ns), 1)

    def column(row):
        return jnp.sum(jnp.where(eye, row, 0.0), axis=-1, keepdims=True)

    def whole(row):
        return column(row.astype(F32)).astype(jnp.int32)

    listed = whole(pages_ref[0:1, :]) == page
    for j in range(1, pages_ref.shape[0]):
        listed = listed | (whole(pages_ref[j : j + 1, :]) == page)
    usable = jnp.where(listed & (pos < whole(lens_ref[0:1, :])), 1.0, 0.0)
    load_q.wait()
    groups = a_buf.shape[0]
    gs = ns // groups
    per = gs * hh_n
    some = gs * nh
    ri = lax.broadcasted_iota(jnp.int32, (some, 1), 0)
    rest = ri & (per - 1)
    origin = (rest >> log2(hh_n)) * nh + (ri >> log2(per)) * hh_n + (rest & (hh_n - 1))
    ci = lax.broadcasted_iota(jnp.int32, (some, some), 1)
    perm = jnp.where(ci == origin, 1.0, 0.0).astype(BF16)

    def a_copy(g, d, slot):
        return to_pool(a_buf.at[g, peer(d)], a_recv.at[g, slot], a_s.at[g, d], a_r.at[g, d], peer(d))

    for g in range(groups):
        streams = range(g * gs, (g + 1) * gs)
        for s in streams:
            load_k[s].wait()
            scores[s] = dot(q[s], cache[s])
        if g == groups - 1:
            for copy in (load_g, load_u, load_d):
                copy.start()
        for s in streams:
            keep = usable[s : s + 1, :] > 0.5
            sc = jnp.where(keep, scores[s] * SCALE, -1e30)
            top = jnp.max(sc, axis=-1, keepdims=True)
            weighed = jnp.where(keep, jnp.exp(sc - top), 0.0)
            probs = (weighed / jnp.sum(weighed, axis=-1, keepdims=True)).astype(BF16)
            lat[s * nh : (s + 1) * nh, :] = lax.dot_general(
                probs, cache[s, :LATENT, :], (((1,), (1,)), ((), ())), preferred_element_type=F32
            ).astype(BF16)
        sent_rows = dot(perm, lat[g * some : (g + 1) * some, :])
        a_buf[g] = sent_rows.reshape(pool, per, LATENT).astype(BF16)
        if g == 0:
            pl.semaphore_wait(barrier, pool)
        each(lambda d: a_copy(g, d, p).start())
        a_recv[g, p] = a_buf[g, p]
    load_vu.wait()
    for g in range(groups):
        each(lambda d: a_copy(g, d, source(d)).wait_recv())
    got = a_recv[...].astype(F32).reshape(rows, LATENT).astype(BF16)
    values = []
    ti = lax.broadcasted_iota(jnp.int32, (toks, 1), 0)
    tj = lax.broadcasted_iota(jnp.int32, (toks, rows), 1)
    for hh in range(hh_n):
        if hh_n > 1:
            inside = ti & (ns - 1)
            spot = (inside >> log2(gs)) * pool + (ti >> log2(ns))
            spot = (spot * gs + (inside & (gs - 1))) * hh_n + hh
            pick = jnp.where(tj == spot, 1.0, 0.0).astype(BF16)
            mine = dot(pick, got).astype(BF16)
        else:
            mine = got
        values.append(dot(mine, vu[hh]).astype(BF16))
    head_values = jnp.concatenate(values, axis=1) if hh_n > 1 else values[0]

    def x_copy(i, c):
        return to_core(x_buf.at[i, c], x_recv.at[i, c], x_s.at[i, c], x_r.at[i, c])

    def y_copy(i, c):
        return to_pool(y_buf.at[i, c, 1 - y], y_recv.at[i, c], y_s.at[i, c], y_r.at[i, c], beside)

    def r_copy(i, c, d, slot):
        return to_pool(
            r_buf.at[i, c, ahead(d)], r_recv.at[i, c, slot], r_s.at[i, c, d], r_r.at[i, c, d],
            ahead(d) * 2 + y,
        )

    def columns(side, c, j=0, size=ck):
        return pl.ds(pl.multiple_of(side * half + (c * ck + j * cq), 128), size)

    def reduce_send(i, lhs, weights, by):
        for c in range(CHUNKS):
            v = dot(lhs, weights[:, columns(oh, c)])
            if by is not None:
                v = v * by
            x_buf[i, c] = v.astype(BF16)
            x_copy(i, c).start()
        for c in range(CHUNKS):
            v = dot(lhs, weights[:, columns(h, c)])
            if by is not None:
                v = v * by
            x_copy(i, c).wait_recv()
            v = v + x_recv[i, c].astype(F32)
            low = v[:, :cq].reshape(lines, 2, ns, cq)
            high = v[:, cq:].reshape(lines, 2, ns, cq)
            for side in range(2):
                y_buf[i, c, side] = jnp.concatenate([low[:, side], high[:, side]], axis=1).astype(BF16)
            y_copy(i, c).start()
        for c in range(CHUNKS):
            y_copy(i, c).wait_recv()
            r_buf[i, c] = (y_buf[i, c, y].astype(F32) + y_recv[i, c].astype(F32)).astype(BF16)
            each(lambda d: r_copy(i, c, d, z).start(), 1, lines)
            r_recv[i, c, z] = r_buf[i, c, z]

    def reduced(i, c):
        each(lambda d: r_copy(i, c, d, behind(d)).wait_recv(), 1, lines)
        return jnp.sum(r_recv[i, c].astype(F32), axis=0)

    load_op.wait()
    reduce_send(0, head_values, op, None)

    load_tok.wait()
    squares = jnp.zeros((ns, 1), F32)
    for c in range(CHUNKS):
        total = reduced(0, c)
        tokens = jnp.concatenate(
            [tok[:, columns(h, c, j, cq)].astype(F32) for j in range(2)], axis=0
        )
        gain = jnp.concatenate(
            [jnp.broadcast_to(gain_ref[0:1, columns(h, c, j, cq)], (ns, cq)) for j in range(2)], axis=0
        )
        res = tokens + total
        resid[c] = res
        both = jnp.sum(res * res, axis=-1, keepdims=True)
        squares = squares + both[:ns] + both[ns:]
        c_recv[h, p, :, c * cq : (c + 1) * cq] = (res * gain).astype(BF16)
    lane = lax.broadcasted_iota(jnp.int32, (ns, 128), 1)
    extra = jnp.broadcast_to(squares, (ns, 128))
    extra = jnp.where(lane < EXPERTS, 0.0, extra)
    for k in range(ids_ref.shape[0]):
        routed = lane == whole(ids_ref[k : k + 1, :])
        extra = extra + jnp.where(routed, column(rw_ref[k : k + 1, :]), 0.0)
    upper = extra.astype(BF16).astype(F32)
    c_recv[h, p, :, block_w:] = jnp.concatenate([upper, extra - upper], axis=0).astype(BF16)

    def c_copy(d, line):
        slot = line * 2 + y
        block = c_recv.at[h, slot]
        return to_pool(block, block, c_s.at[d], c_r.at[d], ahead(d) * 2 + y)

    def g_copy(d, side):
        block = c_recv.at[h, behind(d) * 2 + side]
        return to_pool(block, block, g_s.at[d], g_r.at[d], beside)

    def f_copy(d, far, half_of):
        slot = behind(d) * 2 + (1 - y if far else y)
        block = c_recv.at[half_of, slot]
        return to_core(block, block, f_s.at[far, d], f_r.at[far, d])

    each(lambda d: c_copy(d, z).start(), 1, lines)
    g_copy(0, y).start()
    f_copy(0, 0, h).start()
    load_g.wait()
    load_u.wait()

    def pass_on(d):
        c_copy(d, behind(d)).wait_recv()
        g_copy(d, y).start()
        f_copy(d, 0, h).start()
        g_copy(d - 1, 1 - y).wait_recv()
        f_copy(d - 1, 1, h).start()

    each(pass_on, 1, lines)
    g_copy(lines - 1, 1 - y).wait_recv()
    f_copy(lines - 1, 1, h).start()

    def project(side):
        gate = up = None
        for c in range(CHUNKS):
            part = c_recv[side, :, :, c * cq : (c + 1) * cq].astype(F32)
            x = jnp.concatenate(
                [part[:, j * ns : (j + 1) * ns].reshape(toks, cq) for j in range(2)], axis=1
            ).astype(BF16)
            g = dot(x, gw[columns(side, c), :])
            u = dot(x, uw[columns(side, c), :])
            gate = g if gate is None else gate + g
            up = u if up is None else up + u
        part = c_recv[side, :, :, block_w:].astype(F32)
        return gate, up, (part[:, :ns] + part[:, ns:]).reshape(toks, 128)

    gate0, up0, extra0 = project(h)
    for far in range(2):
        each(lambda d: f_copy(d, far, oh).wait_recv(), 0, lines)
    gate1, up1, extra1 = project(oh)
    lane = lax.broadcasted_iota(jnp.int32, (toks, 128), 1)
    expert = p // (pool // EXPERTS)
    share = jnp.sum(jnp.where(lane == expert, extra0, 0.0), axis=-1, keepdims=True)
    squares = jnp.sum(jnp.where(lane == EXPERTS, extra0 + extra1, 0.0), axis=-1, keepdims=True)
    back = lax.rsqrt(squares / width + 1e-06)
    gate = (gate0 + gate1) * back
    up = (up0 + up1) * back
    act = (gate / (1.0 + jnp.exp(-gate)) * up).astype(BF16)

    load_d.wait()
    reduce_send(1, act, dw, share)
    for c in range(CHUNKS):
        o_buf[h, c] = (resid[c] + reduced(1, c)).astype(BF16)

    def o_copy(side):
        return to_core(o_buf.at[side], o_buf.at[side], o_s.at[0], o_r.at[0])

    o_copy(h).start()

    def sent(d):
        for g in range(groups):
            a_copy(g, d, p).wait_send()

    def sent_line(d):
        c_copy(d, z).wait_send()
        for i in range(2):
            for c in range(CHUNKS):
                r_copy(i, c, d, z).wait_send()

    def sent_near(d):
        g_copy(d, y).wait_send()
        for far in range(2):
            f_copy(d, far, h).wait_send()

    each(sent)
    each(sent_line, 1, lines)
    each(sent_near, 0, lines)
    for i in range(2):
        for c in range(CHUNKS):
            x_copy(i, c).wait_send()
            y_copy(i, c).wait_send()
    o_copy(oh).wait_recv()
    for side in range(2):
        for c in range(CHUNKS):
            part = o_buf[side, c].astype(F32)
            for j in range(2):
                at = side * half + c * ck + j * cq
                out_ref[:, at : at + cq] = part[j * ns : (j + 1) * ns].astype(BF16)
    o_copy(h).wait_send()


def per_device(
    pool,
    tokens, queries, cache_latent, page_lists, cache_lengths, value_up, out_proj, norm_gain,
    expert_ids, route_weights, gate_proj, up_proj, down_proj,
):
    ns, width = tokens.shape
    _, nh, kdim = queries.shape
    ctx = cache_latent.shape[1]
    _, hh_n, latent, vdim = value_up.shape
    hidden = gate_proj.shape[2]
    half = width // 2
    ck = half // CHUNKS
    cq = ck // 2
    toks = pool * ns
    lines = pool // 2
    groups = 2 if ns * hh_n >= 32 else 1
    dma = pltpu.SemaphoreType.DMA
    anywhere = pl.BlockSpec(memory_space=pl.ANY)
    vmem = pl.BlockSpec(memory_space=pltpu.VMEM)
    return pl.pallas_call(
        functools.partial(kernel, pool),
        out_shape=jax.ShapeDtypeStruct((ns, width), BF16),
        in_specs=[
            anywhere, anywhere, anywhere, vmem, vmem, anywhere, anywhere, vmem, vmem, vmem,
            anywhere, anywhere, anywhere,
        ],
        out_specs=vmem,
        scratch_shapes=[
            pltpu.VMEM((ns, width), BF16),
            pltpu.VMEM((ns, nh, kdim), BF16),
            pltpu.VMEM((ns, kdim, ctx), BF16),
            pltpu.VMEM((hh_n, latent, vdim), BF16),
            pltpu.VMEM((hh_n * vdim, width), BF16),
            pltpu.VMEM((width, hidden), BF16),
            pltpu.VMEM((width, hidden), BF16),
            pltpu.VMEM((hidden, width), BF16),
            pltpu.VMEM((ns, nh, ctx), F32),
            pltpu.VMEM((ns * nh, latent), BF16),
            pltpu.VMEM((groups, pool, ns // groups * hh_n, latent), BF16),
            pltpu.VMEM((groups, pool, ns // groups * hh_n, latent), BF16),
            pltpu.VMEM((2, CHUNKS, toks, ck), BF16),
            pltpu.VMEM((2, CHUNKS, toks, ck), BF16),
            pltpu.VMEM((2, CHUNKS, 2, lines, 2 * ns, cq), BF16),
            pltpu.VMEM((2, CHUNKS, lines, 2 * ns, cq), BF16),
            pltpu.VMEM((2, CHUNKS, lines, 2 * ns, cq), BF16),
            pltpu.VMEM((2, CHUNKS, lines, 2 * ns, cq), BF16),
            pltpu.VMEM((2, pool, 2 * ns, CHUNKS * cq + 128), BF16),
            pltpu.VMEM((CHUNKS, 2 * ns, cq), F32),
            pltpu.VMEM((2, CHUNKS, 2 * ns, cq), BF16),
            dma((ns,)), dma((7,)),
            dma((groups, pool)), dma((groups, pool)),
            dma((2, CHUNKS)), dma((2, CHUNKS)),
            dma((2, CHUNKS)), dma((2, CHUNKS)),
            dma((2, CHUNKS, lines)), dma((2, CHUNKS, lines)),
            dma((lines,)), dma((lines,)),
            dma((lines,)), dma((lines,)),
            dma((2, lines)), dma((2, lines)),
            dma((1,)), dma((1,)),
        ],
        compiler_params=pltpu.CompilerParams(
            collective_id=0, has_side_effects=True, vmem_limit_bytes=60 * 1024 * 1024
        ),
        name="decode_layer",
    )(
        tokens, queries, jnp.swapaxes(cache_latent, 1, 2), page_lists.T, cache_lengths.reshape(1, ns),
        value_up.reshape(hh_n, latent, vdim), out_proj.reshape(hh_n * vdim, width),
        norm_gain.reshape(1, width), expert_ids.T, route_weights.T,
        gate_proj.reshape(width, hidden), up_proj.reshape(width, hidden),
        down_proj.reshape(hidden, width),
    )


def solution(mesh):
    return jax.shard_map(
        functools.partial(per_device, mesh.shape["pool"]),
        mesh=mesh,
        in_specs=(
            P(("groups", "pool"), None),
            P(("groups", "pool"), "head", None),
            P(("groups", "pool"), None, None),
            P(("groups", "pool"), None),
            P(("groups", "pool")),
            P("head", "pool", None, None),
            P("head", "pool", None, None),
            P(),
            P(("groups", "pool"), None),
            P(("groups", "pool"), None),
            P("pool", None, "head"),
            P("pool", None, "head"),
            P("pool", "head", None),
        ),
        out_specs=P(("groups", "pool"), None),
        check_vma=False,
    )
```

```python
import functools

import jax
import jax.numpy as jnp
from jax import lax
from jax.experimental import pallas as pl
from jax.experimental.pallas import tpu as pltpu
from jax.sharding import PartitionSpec as P

LATENT = 512
EXPERTS = 4
PAGE = 64
CHUNKS = 7
PARTS = 2
SCALE = 192 ** (-0.5)
MESH = pl.DeviceIdType.MESH
BF16 = jnp.bfloat16
F32 = jnp.float32


def log2(n):
    assert n & (n - 1) == 0
    return n.bit_length() - 1


def dot(a, b):
    return jnp.dot(a, b, preferred_element_type=F32)


def kernel(
    pool,
    tok_hbm, q_hbm, cache_hbm, pages_ref, lens_ref, vu_hbm, op_hbm, gain_ref, ids_ref, rw_ref,
    g_hbm, u_hbm, d_hbm,
    out_ref,
    tok, q, cache, vu, op, gw, uw, dw,
    scores, lat, a_buf, a_recv, x_buf, x_recv, y_buf, y_recv, r_buf, r_recv, c_recv, resid, o_buf,
    k_sem, w_sem, a_s, a_r, x_s, x_r, y_s, y_r, r_s, r_r, c_s, c_r,
    g_s, g_r, f_s, f_r, o_s, o_r,
):
    p = lax.axis_index("pool")
    h = lax.axis_index("head")
    oh = 1 - h
    lines = pool // 2
    z = p // 2
    y = lax.rem(p, 2)
    beside = z * 2 + 1 - y
    ns, nh, _ = q.shape
    ctx = cache.shape[2]
    hh_n = vu.shape[0]
    width = tok.shape[1]
    half = width // 2
    ck = half // CHUNKS
    cq = ck // 2
    rows = ns * nh
    toks = pool * ns
    block_w = CHUNKS * cq

    load_q = pltpu.make_async_copy(q_hbm, q, w_sem.at[0])
    load_q.start()
    load_k = [pltpu.make_async_copy(cache_hbm.at[s], cache.at[s], k_sem.at[s]) for s in range(ns)]
    for copy in load_k:
        copy.start()
    load_vu = pltpu.make_async_copy(vu_hbm, vu, w_sem.at[1])
    load_op = pltpu.make_async_copy(op_hbm, op, w_sem.at[2])
    load_tok = pltpu.make_async_copy(tok_hbm, tok, w_sem.at[3])
    load_g = pltpu.make_async_copy(g_hbm, gw, w_sem.at[4])
    load_u = pltpu.make_async_copy(u_hbm, uw, w_sem.at[5])
    load_d = pltpu.make_async_copy(d_hbm, dw, w_sem.at[6])
    for copy in (load_vu, load_op, load_tok):
        copy.start()

    def peer(d):
        return lax.rem(p + d, pool)

    def source(d):
        return lax.rem(p + pool - d, pool)

    barrier = pltpu.get_barrier_semaphore()

    def greet(d, carry):
        pl.semaphore_signal(barrier, inc=1, device_id={"pool": peer(d)}, device_id_type=MESH)
        return carry

    lax.fori_loop(1, pool, greet, 0)
    pl.semaphore_signal(barrier, inc=1, device_id={"head": oh}, device_id_type=MESH)

    def to_pool(src, dst, send, recv, to):
        return pltpu.make_async_remote_copy(
            src_ref=src, dst_ref=dst, send_sem=send, recv_sem=recv,
            device_id={"pool": to}, device_id_type=MESH,
        )

    def to_core(src, dst, send, recv):
        return pltpu.make_async_remote_copy(
            src_ref=src, dst_ref=dst, send_sem=send, recv_sem=recv,
            device_id={"head": oh}, device_id_type=MESH,
        )

    def each(body, low=1, high=pool):
        def step(d, carry):
            body(d)
            return carry

        lax.fori_loop(low, high, step, 0)

    def ahead(d):
        return lax.rem(z + d, lines)

    def behind(d):
        return lax.rem(z + lines - d, lines)

    pos = lax.broadcasted_iota(jnp.int32, (ns, ctx), 1)
    page = pos >> log2(PAGE)
    eye = lax.broadcasted_iota(jnp.int32, (ns, ns), 0) == lax.broadcasted_iota(jnp.int32, (ns, ns), 1)

    def column(row):
        return jnp.sum(jnp.where(eye, row, 0.0), axis=-1, keepdims=True)

    def whole(row):
        return column(row.astype(F32)).astype(jnp.int32)

    listed = whole(pages_ref[0:1, :]) == page
    for j in range(1, pages_ref.shape[0]):
        listed = listed | (whole(pages_ref[j : j + 1, :]) == page)
    usable = jnp.where(listed & (pos < whole(lens_ref[0:1, :])), 1.0, 0.0)
    load_q.wait()
    groups = a_buf.shape[0]
    gs = ns // groups
    per = gs * hh_n
    some = gs * nh
    ri = lax.broadcasted_iota(jnp.int32, (some, 1), 0)
    rest = ri & (per - 1)
    origin = (rest >> log2(hh_n)) * nh + (ri >> log2(per)) * hh_n + (rest & (hh_n - 1))
    ci = lax.broadcasted_iota(jnp.int32, (some, some), 1)
    perm = jnp.where(ci == origin, 1.0, 0.0).astype(BF16)

    def a_copy(g, d, slot):
        return to_pool(a_buf.at[g, peer(d)], a_recv.at[g, slot], a_s.at[g, d], a_r.at[g, d], peer(d))

    for g in range(groups):
        streams = range(g * gs, (g + 1) * gs)
        for s in streams:
            load_k[s].wait()
            scores[s] = dot(q[s], cache[s])
        if g == groups - 1:
            for copy in (load_g, load_u, load_d):
                copy.start()
        for s in streams:
            keep = usable[s : s + 1, :] > 0.5
            sc = jnp.where(keep, scores[s] * SCALE, -1e30)
            top = jnp.max(sc, axis=-1, keepdims=True)
            weighed = jnp.where(keep, jnp.exp(sc - top), 0.0)
            probs = (weighed / jnp.sum(weighed, axis=-1, keepdims=True)).astype(BF16)
            lat[s * nh : (s + 1) * nh, :] = lax.dot_general(
                probs, cache[s, :LATENT, :], (((1,), (1,)), ((), ())), preferred_element_type=F32
            ).astype(BF16)
        sent_rows = dot(perm, lat[g * some : (g + 1) * some, :])
        a_buf[g] = sent_rows.reshape(pool, per, LATENT).astype(BF16)
        if g == 0:
            pl.semaphore_wait(barrier, pool)
        each(lambda d: a_copy(g, d, p).start())
        a_recv[g, p] = a_buf[g, p]
    load_vu.wait()
    for g in range(groups):
        each(lambda d: a_copy(g, d, source(d)).wait_recv())
    got = a_recv[...].astype(F32).reshape(rows, LATENT).astype(BF16)
    values = []
    ti = lax.broadcasted_iota(jnp.int32, (toks, 1), 0)
    tj = lax.broadcasted_iota(jnp.int32, (toks, rows), 1)
    for hh in range(hh_n):
        if hh_n > 1:
            inside = ti & (ns - 1)
            spot = (inside >> log2(gs)) * pool + (ti >> log2(ns))
            spot = (spot * gs + (inside & (gs - 1))) * hh_n + hh
            pick = jnp.where(tj == spot, 1.0, 0.0).astype(BF16)
            mine = dot(pick, got).astype(BF16)
        else:
            mine = got
        values.append(dot(mine, vu[hh]).astype(BF16))
    head_values = jnp.concatenate(values, axis=1) if hh_n > 1 else values[0]

    def x_copy(i, c):
        return to_core(x_buf.at[i, c], x_recv.at[i, c], x_s.at[i, c], x_r.at[i, c])

    def y_copy(i, c):
        return to_pool(y_buf.at[i, c, 1 - y], y_recv.at[i, c], y_s.at[i, c], y_r.at[i, c], beside)

    def r_copy(i, c, d, slot):
        return to_pool(
            r_buf.at[i, c, ahead(d)], r_recv.at[i, c, slot], r_s.at[i, c, d], r_r.at[i, c, d],
            ahead(d) * 2 + y,
        )

    def columns(side, c, j=0, size=ck):
        return pl.ds(pl.multiple_of(side * half + (c * ck + j * cq), 128), size)

    def reduce_send(i, lhs, weights, by):
        for c in range(CHUNKS):
            v = dot(lhs, weights[:, columns(oh, c)])
            if by is not None:
                v = v * by
            x_buf[i, c] = v.astype(BF16)
            x_copy(i, c).start()
        for c in range(CHUNKS):
            v = dot(lhs, weights[:, columns(h, c)])
            if by is not None:
                v = v * by
            x_copy(i, c).wait_recv()
            v = v + x_recv[i, c].astype(F32)
            low = v[:, :cq].reshape(lines, 2, ns, cq)
            high = v[:, cq:].reshape(lines, 2, ns, cq)
            for side in range(2):
                y_buf[i, c, side] = jnp.concatenate([low[:, side], high[:, side]], axis=1).astype(BF16)
            y_copy(i, c).start()
        for c in range(CHUNKS):
            y_copy(i, c).wait_recv()
            r_buf[i, c] = (y_buf[i, c, y].astype(F32) + y_recv[i, c].astype(F32)).astype(BF16)
            each(lambda d: r_copy(i, c, d, z).start(), 1, lines)
            r_recv[i, c, z] = r_buf[i, c, z]

    def reduced(i, c):
        each(lambda d: r_copy(i, c, d, behind(d)).wait_recv(), 1, lines)
        return jnp.sum(r_recv[i, c].astype(F32), axis=0)

    load_op.wait()
    reduce_send(0, head_values, op, None)

    load_tok.wait()
    squares = jnp.zeros((ns, 1), F32)
    for c in range(CHUNKS):
        total = reduced(0, c)
        tokens = jnp.concatenate(
            [tok[:, columns(h, c, j, cq)].astype(F32) for j in range(2)], axis=0
        )
        gain = jnp.concatenate(
            [jnp.broadcast_to(gain_ref[0:1, columns(h, c, j, cq)], (ns, cq)) for j in range(2)], axis=0
        )
        res = tokens + total
        resid[c] = res
        both = jnp.sum(res * res, axis=-1, keepdims=True)
        squares = squares + both[:ns] + both[ns:]
        c_recv[h, p, :, c * cq : (c + 1) * cq] = (res * gain).astype(BF16)
    lane = lax.broadcasted_iota(jnp.int32, (ns, 128), 1)
    extra = jnp.broadcast_to(squares, (ns, 128))
    extra = jnp.where(lane < EXPERTS, 0.0, extra)
    for k in range(ids_ref.shape[0]):
        routed = lane == whole(ids_ref[k : k + 1, :])
        extra = extra + jnp.where(routed, column(rw_ref[k : k + 1, :]), 0.0)
    upper = extra.astype(BF16).astype(F32)
    c_recv[h, p, :, block_w:] = jnp.concatenate([upper, extra - upper], axis=0).astype(BF16)

    lanes = -(-(block_w + 128) // (PARTS * 128)) * 128
    spans = [pl.ds(k * lanes, min(lanes, block_w + 128 - k * lanes)) for k in range(PARTS)]

    def c_copy(k, d, line):
        block = c_recv.at[h, line * 2 + y, :, spans[k]]
        return to_pool(block, block, c_s.at[k, d], c_r.at[k, d], ahead(d) * 2 + y)

    def g_copy(k, d, side):
        block = c_recv.at[h, behind(d) * 2 + side, :, spans[k]]
        return to_pool(block, block, g_s.at[k, d], g_r.at[k, d], beside)

    def f_copy(k, d, far, half_of):
        block = c_recv.at[half_of, behind(d) * 2 + (1 - y if far else y), :, spans[k]]
        return to_core(block, block, f_s.at[k, far, d], f_r.at[k, far, d])

    for k in range(PARTS):
        each(lambda d: c_copy(k, d, z).start(), 1, lines)
        g_copy(k, 0, y).start()
        f_copy(k, 0, 0, h).start()
    load_g.wait()
    load_u.wait()
    for k in range(PARTS):

        def pass_on(d):
            c_copy(k, d, behind(d)).wait_recv()
            g_copy(k, d, y).start()
            f_copy(k, d, 0, h).start()

        def pass_far(d):
            g_copy(k, d, 1 - y).wait_recv()
            f_copy(k, d, 1, h).start()

        each(pass_on, 1, lines)
        if k > 0:
            last = k - 1

            def pass_last(d):
                g_copy(last, d, 1 - y).wait_recv()
                f_copy(last, d, 1, h).start()

            each(pass_last, 0, lines)
        if k == PARTS - 1:
            each(pass_far, 0, lines)

    def project(side):
        gate = up = None
        for c in range(CHUNKS):
            part = c_recv[side, :, :, c * cq : (c + 1) * cq].astype(F32)
            x = jnp.concatenate(
                [part[:, j * ns : (j + 1) * ns].reshape(toks, cq) for j in range(2)], axis=1
            ).astype(BF16)
            g = dot(x, gw[columns(side, c), :])
            u = dot(x, uw[columns(side, c), :])
            gate = g if gate is None else gate + g
            up = u if up is None else up + u
        part = c_recv[side, :, :, block_w:].astype(F32)
        return gate, up, (part[:, :ns] + part[:, ns:]).reshape(toks, 128)

    gate0, up0, extra0 = project(h)
    for k in range(PARTS):
        for far in range(2):
            each(lambda d: f_copy(k, d, far, oh).wait_recv(), 0, lines)
    gate1, up1, extra1 = project(oh)
    lane = lax.broadcasted_iota(jnp.int32, (toks, 128), 1)
    expert = p // (pool // EXPERTS)
    share = jnp.sum(jnp.where(lane == expert, extra0, 0.0), axis=-1, keepdims=True)
    squares = jnp.sum(jnp.where(lane == EXPERTS, extra0 + extra1, 0.0), axis=-1, keepdims=True)
    back = lax.rsqrt(squares / width + 1e-06)
    gate = (gate0 + gate1) * back
    up = (up0 + up1) * back
    act = (gate / (1.0 + jnp.exp(-gate)) * up).astype(BF16)

    load_d.wait()
    reduce_send(1, act, dw, share)
    for c in range(CHUNKS):
        o_buf[h, c] = (resid[c] + reduced(1, c)).astype(BF16)

    def o_copy(side):
        return to_core(o_buf.at[side], o_buf.at[side], o_s.at[0], o_r.at[0])

    o_copy(h).start()

    def sent(d):
        for g in range(groups):
            a_copy(g, d, p).wait_send()

    def sent_line(d):
        for k in range(PARTS):
            c_copy(k, d, z).wait_send()
        for i in range(2):
            for c in range(CHUNKS):
                r_copy(i, c, d, z).wait_send()

    def sent_near(d):
        for k in range(PARTS):
            g_copy(k, d, y).wait_send()
            for far in range(2):
                f_copy(k, d, far, h).wait_send()

    each(sent)
    each(sent_line, 1, lines)
    each(sent_near, 0, lines)
    for i in range(2):
        for c in range(CHUNKS):
            x_copy(i, c).wait_send()
            y_copy(i, c).wait_send()
    o_copy(oh).wait_recv()
    for side in range(2):
        for c in range(CHUNKS):
            part = o_buf[side, c].astype(F32)
            for j in range(2):
                at = side * half + c * ck + j * cq
                out_ref[:, at : at + cq] = part[j * ns : (j + 1) * ns].astype(BF16)
    o_copy(h).wait_send()


def per_device(
    pool,
    tokens, queries, cache_latent, page_lists, cache_lengths, value_up, out_proj, norm_gain,
    expert_ids, route_weights, gate_proj, up_proj, down_proj,
):
    ns, width = tokens.shape
    _, nh, kdim = queries.shape
    ctx = cache_latent.shape[1]
    _, hh_n, latent, vdim = value_up.shape
    hidden = gate_proj.shape[2]
    half = width // 2
    ck = half // CHUNKS
    cq = ck // 2
    toks = pool * ns
    lines = pool // 2
    groups = 2 if ns * hh_n >= 32 else 1
    dma = pltpu.SemaphoreType.DMA
    anywhere = pl.BlockSpec(memory_space=pl.ANY)
    vmem = pl.BlockSpec(memory_space=pltpu.VMEM)
    return pl.pallas_call(
        functools.partial(kernel, pool),
        out_shape=jax.ShapeDtypeStruct((ns, width), BF16),
        in_specs=[
            anywhere, anywhere, anywhere, vmem, vmem, anywhere, anywhere, vmem, vmem, vmem,
            anywhere, anywhere, anywhere,
        ],
        out_specs=vmem,
        scratch_shapes=[
            pltpu.VMEM((ns, width), BF16),
            pltpu.VMEM((ns, nh, kdim), BF16),
            pltpu.VMEM((ns, kdim, ctx), BF16),
            pltpu.VMEM((hh_n, latent, vdim), BF16),
            pltpu.VMEM((hh_n * vdim, width), BF16),
            pltpu.VMEM((width, hidden), BF16),
            pltpu.VMEM((width, hidden), BF16),
            pltpu.VMEM((hidden, width), BF16),
            pltpu.VMEM((ns, nh, ctx), F32),
            pltpu.VMEM((ns * nh, latent), BF16),
            pltpu.VMEM((groups, pool, ns // groups * hh_n, latent), BF16),
            pltpu.VMEM((groups, pool, ns // groups * hh_n, latent), BF16),
            pltpu.VMEM((2, CHUNKS, toks, ck), BF16),
            pltpu.VMEM((2, CHUNKS, toks, ck), BF16),
            pltpu.VMEM((2, CHUNKS, 2, lines, 2 * ns, cq), BF16),
            pltpu.VMEM((2, CHUNKS, lines, 2 * ns, cq), BF16),
            pltpu.VMEM((2, CHUNKS, lines, 2 * ns, cq), BF16),
            pltpu.VMEM((2, CHUNKS, lines, 2 * ns, cq), BF16),
            pltpu.VMEM((2, pool, 2 * ns, CHUNKS * cq + 128), BF16),
            pltpu.VMEM((CHUNKS, 2 * ns, cq), F32),
            pltpu.VMEM((2, CHUNKS, 2 * ns, cq), BF16),
            dma((ns,)), dma((7,)),
            dma((groups, pool)), dma((groups, pool)),
            dma((2, CHUNKS)), dma((2, CHUNKS)),
            dma((2, CHUNKS)), dma((2, CHUNKS)),
            dma((2, CHUNKS, lines)), dma((2, CHUNKS, lines)),
            dma((PARTS, lines)), dma((PARTS, lines)),
            dma((PARTS, lines)), dma((PARTS, lines)),
            dma((PARTS, 2, lines)), dma((PARTS, 2, lines)),
            dma((1,)), dma((1,)),
        ],
        compiler_params=pltpu.CompilerParams(
            collective_id=0, has_side_effects=True, vmem_limit_bytes=60 * 1024 * 1024
        ),
        name="decode_layer",
    )(
        tokens, queries, jnp.swapaxes(cache_latent, 1, 2), page_lists.T, cache_lengths.reshape(1, ns),
        value_up.reshape(hh_n, latent, vdim), out_proj.reshape(hh_n * vdim, width),
        norm_gain.reshape(1, width), expert_ids.T, route_weights.T,
        gate_proj.reshape(width, hidden), up_proj.reshape(width, hidden),
        down_proj.reshape(hidden, width),
    )


def solution(mesh):
    return jax.shard_map(
        functools.partial(per_device, mesh.shape["pool"]),
        mesh=mesh,
        in_specs=(
            P(("groups", "pool"), None),
            P(("groups", "pool"), "head", None),
            P(("groups", "pool"), None, None),
            P(("groups", "pool"), None),
            P(("groups", "pool")),
            P("head", "pool", None, None),
            P("head", "pool", None, None),
            P(),
            P(("groups", "pool"), None),
            P(("groups", "pool"), None),
            P("pool", None, "head"),
            P("pool", None, "head"),
            P("pool", "head", None),
        ),
        out_specs=P(("groups", "pool"), None),
        check_vma=False,
    )
```
